32 devices in a mesh: blk: 8 (over z, x), col: 4 (over y, core).
Axes of the slice: x: 2, y: 2, z: 4, core: 2. Of those that a mesh axis runs over, the one named last changes fastest.
Arguments:
- density: float32 [2048, 1024], P('blk'), may hold values from -0.1875 to 0.1875
- occupied_p: int32 [16, 8], P('blk'), may hold values 0 or 1
- hamil_dens: float32 [1024, 2048], P('blk', 'col'), may hold values from -6 to 6
- occupied_hp: int32 [8, 16], P('blk', 'col'), may hold values 0 or 1
- window_sizes: int32 [8], replicated, may hold values from 64 to 128
- row_window_sizes: int32 [16], replicated, may hold values from 64 to 128
- slab_index: int32 [16], P('col'), may hold values from 0 to 781
- group_sizes: int32 [782], replicated, may hold values from 64 to 128
Outputs:
- product: float32 [2048, 2048], P('blk', 'col')
- norm_sq: float32 [], replicated
The draws below stay inside these ranges and needn't reach their ends.
All inputs are finite; a program needn't handle non-finite values. No bound on the sum of `occupied_p` or of `occupied_hp` on one device may be relied on, other than what follows from the above.
Results may differ from the reference program's by a relative error of at most 0.000068.
Values sent between devices are 32-bit elements; how exact they have to be, the bound alone decides.
A program may use at most 64 MiB of HBM per device.

```python
import jax
import jax.numpy as jnp
from jax import lax

BS = 128
NGROUP = 782
NB = 8
NR = 16
SC = 16


def with_ends(result, own_key, low, high):
    extent = result.shape
    index_at = [jax.random.randint(jax.random.fold_in(own_key, axis), (), 0, extent[axis]) for axis in range(len(extent))]
    result = result.at[tuple(index_at)].set(low)
    longest = extent.index(max(extent))
    index_at[longest] = (index_at[longest] + 1) % extent[longest]
    return result.at[tuple(index_at)].set(high)


def level_of(own_key, dims, cuts, low, high):
    gain, own = 1.0, jax.random.fold_in(own_key, 6)
    for position, blocks in cuts:
        heights = jnp.exp(jax.random.uniform(jax.random.fold_in(own, position), (blocks,), jnp.float32, low / len(cuts), high / len(cuts)))
        gain = gain * jnp.repeat(heights, dims[position] // blocks).reshape([-1 if axis == position else 1 for axis in range(len(dims))])
    return gain


def bell_draw(own_key, extent, spread, limit, pieces=(), kind=jnp.bfloat16):
    factor_of = level_of(own_key, extent, pieces, -0.22, 0.18) if pieces else 1.0
    result = jax.random.normal(own_key, extent, jnp.float32) * spread * factor_of
    return jnp.minimum(jnp.maximum(result, -limit), limit).astype(kind)


def setup_inputs(seed: int = 0) -> dict:
    key_list = jax.random.split(jax.random.key(seed), 9)
    return {
        "density": bell_draw(key_list[0], (NR * BS, NB * BS), (NB * BS) ** -0.5, 0.1875, ((0, 8),), jnp.float32),
        "occupied_p": with_ends((jax.random.randint(key_list[1], (NR, NB), 0, 2) < 1).astype(jnp.int32), jax.random.fold_in(key_list[1], 1), 0, 1),
        "hamil_dens": bell_draw(key_list[2], (NB * BS, SC * BS), 1.0, 6.0, ((0, 8), (1, 4)), jnp.float32),
        "occupied_hp": with_ends((jax.random.randint(key_list[3], (NB, SC), 0, 2) < 1).astype(jnp.int32), jax.random.fold_in(key_list[3], 1), 0, 1),
        "window_sizes": with_ends(jax.random.randint(key_list[4], (NB,), BS // 2, BS + 1), jax.random.fold_in(key_list[4], 1), BS // 2, BS).astype(jnp.int32),
        "row_window_sizes": with_ends(jax.random.randint(key_list[5], (NR,), BS // 2, BS + 1), jax.random.fold_in(key_list[5], 1), BS // 2, BS).astype(jnp.int32),
        "slab_index": with_ends(jax.random.randint(key_list[6], (SC,), 0, NGROUP), jax.random.fold_in(key_list[6], 1), 0, NGROUP - 1).astype(jnp.int32),
        "group_sizes": with_ends(jax.random.randint(key_list[7], (NGROUP,), BS // 2, BS + 1), jax.random.fold_in(key_list[7], 1), BS // 2, BS).astype(jnp.int32),
    }


def reference(density, occupied_p, hamil_dens, occupied_hp, window_sizes, row_window_sizes, slab_index, group_sizes):
    offsets = jnp.arange(BS, dtype=jnp.int32)
    row_live = (offsets[None, :] < row_window_sizes[:, None]).astype(jnp.float32).reshape(-1)
    inner_live = (offsets[None, :] < window_sizes[:, None]).astype(jnp.float32).reshape(-1)
    slab_sizes = group_sizes[slab_index]
    col_live = (offsets[None, :] < slab_sizes[:, None]).astype(jnp.float32).reshape(-1)
    occ_p = jnp.repeat(jnp.repeat(occupied_p.astype(jnp.float32), BS, axis=0), BS, axis=1)
    occ_hp = jnp.repeat(jnp.repeat(occupied_hp.astype(jnp.float32), BS, axis=0), BS, axis=1)
    p_eff = density * occ_p * row_live[:, None] * inner_live[None, :]
    hp_eff = hamil_dens * occ_hp * inner_live[:, None] * col_live[None, :]
    product = jnp.dot(p_eff, hp_eff, precision=lax.Precision.HIGHEST, preferred_element_type=jnp.float32)
    norm_sq = jnp.sum(product * product)
    return product, norm_sq
```

```python
import functools

import jax
import jax.numpy as jnp
from jax import lax
from jax.experimental import pallas as pl
from jax.experimental.pallas import tpu as pltpu
from jax.sharding import PartitionSpec as P

MESH = pl.DeviceIdType.MESH
PAIR = 2
CHUNKS = 2
EXTRA = 1


def kernel(
    length,
    cols,
    density,
    hamil,
    occ_p,
    occ_hp,
    window,
    row_window,
    slab,
    groups,
    product,
    norm,
    gathered,
    p_in,
    p_high,
    p_low,
    parts,
    col_parts,
    send_sem,
    recv_sem,
    load_sem,
    part_send,
    part_recv,
    col_send,
    col_recv,
):
    count = length * PAIR
    block, width = hamil.shape
    row_blocks = product.shape[0] // block
    panels = width // block
    piece = block // CHUNKS
    me = lax.axis_index("blk")
    my_col = lax.axis_index("col")
    z = me // PAIR
    x = me % PAIR
    partner = me + 1 - 2 * x
    has_up = z < length - 1
    has_down = z > 0

    load = pltpu.make_async_copy(density, p_in, load_sem)
    load.start()

    barrier = pltpu.get_barrier_semaphore()

    @pl.loop(1, count)
    def greet_blk(step):
        pl.semaphore_signal(
            barrier, inc=1, device_id={"blk": (me + step) % count}, device_id_type=MESH
        )

    @pl.loop(1, cols)
    def greet_col(step):
        pl.semaphore_signal(
            barrier, inc=1, device_id={"col": (my_col + step) % cols}, device_id_type=MESH
        )

    row_at = lax.broadcasted_iota(jnp.int32, (block, block), 0)
    col_at = lax.broadcasted_iota(jnp.int32, (block, block), 1)
    rows_live = row_at < window[me]
    for panel in range(panels):
        size = groups[slab[panel]]
        occupied = occ_hp[0, panel].astype(jnp.float32)
        mask = jnp.where(rows_live & (col_at < size), occupied, 0.0)
        here = pl.ds(panel * block, block)
        gathered[me, :, here] = hamil[:, here] * mask

    pl.semaphore_wait(barrier, count - 1 + cols - 1)

    def move(where, k, chunk, device):
        rows = gathered.at[k, pl.ds(chunk * piece, piece), :]
        return pltpu.make_async_remote_copy(
            src_ref=rows,
            dst_ref=rows,
            send_sem=send_sem.at[where, k, chunk],
            recv_sem=recv_sem.at[k, chunk],
            device_id={"blk": device},
            device_id_type=MESH,
        )

    def up(k, chunk):
        return move(0, k, chunk, me + PAIR)

    def down(k, chunk):
        return move(1, k, chunk, me - PAIR)

    def across(k, chunk):
        return move(2, k, chunk, partner)

    for chunk in range(CHUNKS):
        across(me, chunk).start()

        @pl.when(has_up)
        def _():
            up(me, chunk).start()

        @pl.when(has_down)
        def _():
            down(me, chunk).start()

    load.wait()

    @pl.loop(0, length)
    def split(at):
        for b in range(row_blocks):
            live = row_at < row_window[me * row_blocks + b]
            here = pl.ds(b * block, block)
            for other in range(PAIR):
                k = at * PAIR + other
                mask = jnp.where(
                    live & (col_at < window[k]), occ_p[b, k].astype(jnp.float32), 0.0
                )
                value = p_in[here, pl.ds(pl.multiple_of(k * block, block), block)] * mask
                high = value.astype(jnp.bfloat16)
                there = pl.ds(other * block, block)
                p_high[at, here, there] = high
                p_low[at, here, there] = (value - high.astype(jnp.float32)).astype(jnp.bfloat16)

    def term(at, first):
        right = gathered[pl.ds(at * PAIR, PAIR)].reshape(PAIR * block, width)
        high = right.astype(jnp.bfloat16)
        low = (right - high.astype(jnp.float32)).astype(jnp.bfloat16)

        def times(a, b):
            return jnp.dot(a, b, preferred_element_type=jnp.float32)

        left = p_high[at]
        value = times(left, low) + times(p_low[at], high) + times(left, high)
        product[...] = value if first else product[...] + value

    for chunk in range(CHUNKS):
        across(partner, chunk).wait_recv()
        if chunk < EXTRA:

            @pl.when(has_up)
            def _():
                up(partner, chunk).start()

            @pl.when(has_down)
            def _():
                down(partner, chunk).start()

    term(z, True)

    def pass_on(distance):
        for chunk in range(CHUNKS):

            @pl.when(z - distance >= 0)
            def _():
                k = me - distance * PAIR
                across(k, chunk).wait_recv()

                @pl.when(has_up)
                def _():
                    up(k, chunk).start()

                if chunk < EXTRA:

                    @pl.when(distance > 1)
                    def _():
                        across(k, chunk).start()

                else:
                    across(k, chunk).start()

            @pl.when(z + distance < length)
            def _():
                k = me + distance * PAIR
                across(k, chunk).wait_recv()

                @pl.when(has_down)
                def _():
                    down(k, chunk).start()

                if chunk < EXTRA:

                    @pl.when(distance > 1)
                    def _():
                        across(k, chunk).start()

                else:
                    across(k, chunk).start()

    def add_terms(distance):
        for sign in (-1, 1):
            at = z + sign * distance

            @pl.when((at >= 0) & (at < length))
            def _():
                for chunk in range(CHUNKS):
                    across(partner + sign * distance * PAIR, chunk).wait_recv()
                term(at, False)

    if length > 1:
        pass_on(1)

    @pl.loop(2, length)
    def steps(distance):
        pass_on(distance)
        add_terms(distance - 1)

    if length > 1:
        add_terms(length - 1)

    squares = product[...] * product[...]
    squares = jnp.sum(squares.reshape(squares.shape[0] // 8, 8, width), axis=0)
    total = squares[:, :128]
    for panel in range(1, width // 128):
        total = total + squares[:, panel * 128 : (panel + 1) * 128]
    parts[me] = total

    def part_to(device):
        return pltpu.make_async_remote_copy(
            src_ref=parts.at[me],
            dst_ref=parts.at[me],
            send_sem=part_send.at[device],
            recv_sem=part_recv.at[me],
            device_id={"blk": device},
            device_id_type=MESH,
        )

    def part_from(device):
        return pltpu.make_async_remote_copy(
            src_ref=parts.at[device],
            dst_ref=parts.at[device],
            send_sem=part_send.at[device],
            recv_sem=part_recv.at[device],
            device_id={"blk": device},
            device_id_type=MESH,
        )

    @pl.loop(1, count)
    def send_parts(step):
        part_to((me + step) % count).start()

    @pl.loop(0, length)
    def sent(at):
        k = at * PAIR + x
        far = (at - z > 1) | (z - at > 1) | (at == z)
        for chunk in range(CHUNKS):

            @pl.when(has_up & (at <= z))
            def _():
                up(k, chunk).wait_send()

            @pl.when(has_down & (at >= z))
            def _():
                down(k, chunk).wait_send()

            if chunk < EXTRA:

                @pl.when(far)
                def _():
                    across(k, chunk).wait_send()

            else:
                across(k, chunk).wait_send()

    for chunk in range(EXTRA):

        @pl.when(has_up)
        def _():
            up(partner, chunk).wait_send()

        @pl.when(has_down)
        def _():
            down(partner, chunk).wait_send()

    @pl.loop(1, count)
    def get_parts(step):
        part_from((me + step) % count).wait_recv()

    col_parts[my_col] = jnp.sum(parts[...], axis=0)

    def col_to(device):
        return pltpu.make_async_remote_copy(
            src_ref=col_parts.at[my_col],
            dst_ref=col_parts.at[my_col],
            send_sem=col_send.at[device],
            recv_sem=col_recv.at[my_col],
            device_id={"col": device},
            device_id_type=MESH,
        )

    def col_from(device):
        return pltpu.make_async_remote_copy(
            src_ref=col_parts.at[device],
            dst_ref=col_parts.at[device],
            send_sem=col_send.at[device],
            recv_sem=col_recv.at[device],
            device_id={"col": device},
            device_id_type=MESH,
        )

    @pl.loop(1, cols)
    def send_cols(step):
        col_to((my_col + step) % cols).start()

    @pl.loop(1, count)
    def sent_parts(step):
        part_to((me + step) % count).wait_send()

    @pl.loop(1, cols)
    def get_cols(step):
        col_from((my_col + step) % cols).wait_recv()

    norm[0] = jnp.sum(jnp.sum(col_parts[...], axis=0))

    @pl.loop(1, cols)
    def sent_cols(step):
        col_to((my_col + step) % cols).wait_send()


def solution(mesh):
    count = mesh.shape["blk"]
    cols = mesh.shape["col"]
    length = count // PAIR

    def per_device(
        density,
        occupied_p,
        hamil_dens,
        occupied_hp,
        window_sizes,
        row_window_sizes,
        slab_index,
        group_sizes,
    ):
        rows, inner = density.shape
        block, width = hamil_dens.shape
        vmem = pl.BlockSpec(memory_space=pltpu.VMEM)
        smem = pl.BlockSpec(memory_space=pltpu.SMEM)
        product, norm = pl.pallas_call(
            functools.partial(kernel, length, cols),
            out_shape=(
                jax.ShapeDtypeStruct((rows, width), jnp.float32),
                jax.ShapeDtypeStruct((1,), jnp.float32),
            ),
            in_specs=[pl.BlockSpec(memory_space=pltpu.HBM), vmem] + [smem] * 6,
            out_specs=(vmem, smem),
            scratch_shapes=[
                pltpu.VMEM((count, block, width), jnp.float32),
                pltpu.VMEM((rows, inner), jnp.float32),
                pltpu.VMEM((length, rows, PAIR * block), jnp.bfloat16),
                pltpu.VMEM((length, rows, PAIR * block), jnp.bfloat16),
                pltpu.VMEM((count, 8, 128), jnp.float32),
                pltpu.VMEM((cols, 8, 128), jnp.float32),
                pltpu.SemaphoreType.DMA((3, count, CHUNKS)),
                pltpu.SemaphoreType.DMA((count, CHUNKS)),
                pltpu.SemaphoreType.DMA,
                pltpu.SemaphoreType.DMA((count,)),
                pltpu.SemaphoreType.DMA((count,)),
                pltpu.SemaphoreType.DMA((cols,)),
                pltpu.SemaphoreType.DMA((cols,)),
            ],
            compiler_params=pltpu.CompilerParams(
                collective_id=0, has_side_effects=True, vmem_limit_bytes=48 << 20
            ),
        )(
            density,
            hamil_dens,
            occupied_p,
            occupied_hp,
            window_sizes,
            row_window_sizes,
            slab_index,
            group_sizes,
        )
        return product, norm.reshape(())

    return jax.shard_map(
        per_device,
        mesh=mesh,
        in_specs=(
            P("blk", None),
            P("blk", None),
            P("blk", "col"),
            P("blk", "col"),
            P(),
            P(),
            P("col"),
            P(),
        ),
        out_specs=(P("blk", "col"), P()),
        check_vma=False,
    )
```

```python
import functools

import jax
import jax.numpy as jnp
from jax import lax
from jax.experimental import pallas as pl
from jax.experimental.pallas import tpu as pltpu
from jax.sharding import PartitionSpec as P

MESH = pl.DeviceIdType.MESH
PAIR = 2
CHUNKS = 4
EXTRA = 1


def kernel(
    length,
    cols,
    density,
    hamil_in,
    occ_p_in,
    occ_hp_in,
    window_in,
    row_window_in,
    slab_in,
    groups_in,
    product_out,
    norm,
    product,
    hamil,
    occ_p,
    occ_hp,
    window,
    row_window,
    slab,
    groups,
    gathered,
    p_in,
    p_high,
    p_low,
    parts,
    col_parts,
    send_sem,
    recv_sem,
    load_sem,
    part_send,
    part_recv,
    col_send,
    col_recv,
):
    count = length * PAIR
    block, width = hamil.shape
    row_blocks = product.shape[0] // block
    panels = width // block
    piece = block // CHUNKS
    me = lax.axis_index("blk")
    my_col = lax.axis_index("col")
    z = me // PAIR
    x = me % PAIR
    partner = me + 1 - 2 * x
    has_up = z < length - 1
    has_down = z > 0

    loads = [
        pltpu.make_async_copy(source, target, load_sem.at[at])
        for at, (source, target) in enumerate(
            (
                (hamil_in, hamil),
                (occ_hp_in, occ_hp),
                (window_in, window),
                (slab_in, slab),
                (groups_in, groups),
                (row_window_in, row_window),
                (occ_p_in, occ_p),
                (density, p_in),
            )
        )
    ]
    barrier = pltpu.get_barrier_semaphore()

    @pl.loop(1, count)
    def greet_blk(step):
        pl.semaphore_signal(
            barrier, inc=1, device_id={"blk": (me + step) % count}, device_id_type=MESH
        )

    @pl.loop(1, cols)
    def greet_col(step):
        pl.semaphore_signal(
            barrier, inc=1, device_id={"col": (my_col + step) % cols}, device_id_type=MESH
        )

    for load in loads:
        load.start()

    for load in loads[:5]:
        load.wait()

    row_at = lax.broadcasted_iota(jnp.int32, (block, block), 0)
    col_at = lax.broadcasted_iota(jnp.int32, (block, block), 1)
    rows_live = row_at < window[me]
    for panel in range(panels):
        size = groups[slab[panel]]
        occupied = occ_hp[0, panel].astype(jnp.float32)
        mask = jnp.where(rows_live & (col_at < size), occupied, 0.0)
        here = pl.ds(panel * block, block)
        gathered[me, :, here] = hamil[:, here] * mask

    pl.semaphore_wait(barrier, count - 1 + cols - 1)

    def move(where, k, chunk, device):
        rows = gathered.at[k, pl.ds(chunk * piece, piece), :]
        return pltpu.make_async_remote_copy(
            src_ref=rows,
            dst_ref=rows,
            send_sem=send_sem.at[where, k, chunk],
            recv_sem=recv_sem.at[k, chunk],
            device_id={"blk": device},
            device_id_type=MESH,
        )

    def up(k, chunk):
        return move(0, k, chunk, me + PAIR)

    def down(k, chunk):
        return move(1, k, chunk, me - PAIR)

    def across(k, chunk):
        return move(2, k, chunk, partner)

    for chunk in range(CHUNKS):
        across(me, chunk).start()

        @pl.when(has_up)
        def _():
            up(me, chunk).start()

        @pl.when(has_down)
        def _():
            down(me, chunk).start()

    for load in loads[5:]:
        load.wait()

    @pl.loop(0, length)
    def split(at):
        for b in range(row_blocks):
            live = row_at < row_window[me * row_blocks + b]
            here = pl.ds(b * block, block)
            for other in range(PAIR):
                k = at * PAIR + other
                mask = jnp.where(
                    live & (col_at < window[k]), occ_p[b, k].astype(jnp.float32), 0.0
                )
                value = p_in[here, pl.ds(pl.multiple_of(k * block, block), block)] * mask
                high = value.astype(jnp.bfloat16)
                there = pl.ds(other * block, block)
                p_high[at, here, there] = high
                p_low[at, here, there] = (value - high.astype(jnp.float32)).astype(jnp.bfloat16)

    def term(at, first):
        right = gathered[pl.ds(at * PAIR, PAIR)].reshape(PAIR * block, width)
        high = right.astype(jnp.bfloat16)
        low = (right - high.astype(jnp.float32)).astype(jnp.bfloat16)

        def times(a, b):
            return jnp.dot(a, b, preferred_element_type=jnp.float32)

        left = p_high[at]
        value = times(left, low) + times(p_low[at], high) + times(left, high)
        product[...] = value if first else product[...] + value

    for chunk in range(CHUNKS):
        across(partner, chunk).wait_recv()
        if chunk < EXTRA:

            @pl.when(has_up)
            def _():
                up(partner, chunk).start()

            @pl.when(has_down)
            def _():
                down(partner, chunk).start()

    term(z, True)

    def pass_on(distance):
        for chunk in range(CHUNKS):

            @pl.when(z - distance >= 0)
            def _():
                k = me - distance * PAIR
                across(k, chunk).wait_recv()

                @pl.when(has_up)
                def _():
                    up(k, chunk).start()

                if chunk < EXTRA:

                    @pl.when(distance > 1)
                    def _():
                        across(k, chunk).start()

                else:
                    across(k, chunk).start()

            @pl.when(z + distance < length)
            def _():
                k = me + distance * PAIR
                across(k, chunk).wait_recv()

                @pl.when(has_down)
                def _():
                    down(k, chunk).start()

                if chunk < EXTRA:

                    @pl.when(distance > 1)
                    def _():
                        across(k, chunk).start()

                else:
                    across(k, chunk).start()

    def add_terms(distance):
        for sign in (-1, 1):
            at = z + sign * distance

            @pl.when((at >= 0) & (at < length))
            def _():
                for chunk in range(CHUNKS):
                    across(partner + sign * distance * PAIR, chunk).wait_recv()
                term(at, False)

    if length > 1:
        pass_on(1)

    @pl.loop(2, length)
    def steps(distance):
        pass_on(distance)
        add_terms(distance - 1)

    if length > 1:
        add_terms(length - 1)

    store = pltpu.make_async_copy(product, product_out, load_sem.at[0])
    store.start()

    squares = product[...] * product[...]
    squares = jnp.sum(squares.reshape(squares.shape[0] // 8, 8, width), axis=0)
    total = squares[:, :128]
    for panel in range(1, width // 128):
        total = total + squares[:, panel * 128 : (panel + 1) * 128]
    parts[me] = total

    def part_to(device):
        return pltpu.make_async_remote_copy(
            src_ref=parts.at[me],
            dst_ref=parts.at[me],
            send_sem=part_send.at[device],
            recv_sem=part_recv.at[me],
            device_id={"blk": device},
            device_id_type=MESH,
        )

    def part_from(device):
        return pltpu.make_async_remote_copy(
            src_ref=parts.at[device],
            dst_ref=parts.at[device],
            send_sem=part_send.at[device],
            recv_sem=part_recv.at[device],
            device_id={"blk": device},
            device_id_type=MESH,
        )

    @pl.loop(1, count)
    def send_parts(step):
        part_to((me + step) % count).start()

    @pl.loop(0, length)
    def sent(at):
        k = at * PAIR + x
        far = (at - z > 1) | (z - at > 1) | (at == z)
        for chunk in range(CHUNKS):

            @pl.when(has_up & (at <= z))
            def _():
                up(k, chunk).wait_send()

            @pl.when(has_down & (at >= z))
            def _():
                down(k, chunk).wait_send()

            if chunk < EXTRA:

                @pl.when(far)
                def _():
                    across(k, chunk).wait_send()

            else:
                across(k, chunk).wait_send()

    for chunk in range(EXTRA):

        @pl.when(has_up)
        def _():
            up(partner, chunk).wait_send()

        @pl.when(has_down)
        def _():
            down(partner, chunk).wait_send()

    @pl.loop(1, count)
    def get_parts(step):
        part_from((me + step) % count).wait_recv()

    col_parts[my_col] = jnp.sum(parts[...], axis=0)

    def col_to(device):
        return pltpu.make_async_remote_copy(
            src_ref=col_parts.at[my_col],
            dst_ref=col_parts.at[my_col],
            send_sem=col_send.at[device],
            recv_sem=col_recv.at[my_col],
            device_id={"col": device},
            device_id_type=MESH,
        )

    def col_from(device):
        return pltpu.make_async_remote_copy(
            src_ref=col_parts.at[device],
            dst_ref=col_parts.at[device],
            send_sem=col_send.at[device],
            recv_sem=col_recv.at[device],
            device_id={"col": device},
            device_id_type=MESH,
        )

    @pl.loop(1, cols)
    def send_cols(step):
        col_to((my_col + step) % cols).start()

    @pl.loop(1, count)
    def sent_parts(step):
        part_to((me + step) % count).wait_send()

    @pl.loop(1, cols)
    def get_cols(step):
        col_from((my_col + step) % cols).wait_recv()

    store.wait()
    norm[0] = jnp.sum(jnp.sum(col_parts[...], axis=0))

    @pl.loop(1, cols)
    def sent_cols(step):
        col_to((my_col + step) % cols).wait_send()


def solution(mesh):
    count = mesh.shape["blk"]
    cols = mesh.shape["col"]
    length = count // PAIR

    def per_device(
        density,
        occupied_p,
        hamil_dens,
        occupied_hp,
        window_sizes,
        row_window_sizes,
        slab_index,
        group_sizes,
    ):
        rows, inner = density.shape
        block, width = hamil_dens.shape
        hbm = pl.BlockSpec(memory_space=pltpu.HBM)
        smem = pl.BlockSpec(memory_space=pltpu.SMEM)
        product, norm = pl.pallas_call(
            functools.partial(kernel, length, cols),
            out_shape=(
                jax.ShapeDtypeStruct((rows, width), jnp.float32),
                jax.ShapeDtypeStruct((1,), jnp.float32),
            ),
            in_specs=[hbm] * 8,
            out_specs=(hbm, smem),
            scratch_shapes=[
                pltpu.VMEM((rows, width), jnp.float32),
                pltpu.VMEM((block, width), jnp.float32),
                pltpu.SMEM(occupied_p.shape, jnp.int32),
                pltpu.SMEM(occupied_hp.shape, jnp.int32),
                pltpu.SMEM(window_sizes.shape, jnp.int32),
                pltpu.SMEM(row_window_sizes.shape, jnp.int32),
                pltpu.SMEM(slab_index.shape, jnp.int32),
                pltpu.SMEM(group_sizes.shape, jnp.int32),
                pltpu.VMEM((count, block, width), jnp.float32),
                pltpu.VMEM((rows, inner), jnp.float32),
                pltpu.VMEM((length, rows, PAIR * block), jnp.bfloat16),
                pltpu.VMEM((length, rows, PAIR * block), jnp.bfloat16),
                pltpu.VMEM((count, 8, 128), jnp.float32),
                pltpu.VMEM((cols, 8, 128), jnp.float32),
                pltpu.SemaphoreType.DMA((3, count, CHUNKS)),
                pltpu.SemaphoreType.DMA((count, CHUNKS)),
                pltpu.SemaphoreType.DMA((8,)),
                pltpu.SemaphoreType.DMA((count,)),
                pltpu.SemaphoreType.DMA((count,)),
                pltpu.SemaphoreType.DMA((cols,)),
                pltpu.SemaphoreType.DMA((cols,)),
            ],
            compiler_params=pltpu.CompilerParams(
                collective_id=0, has_side_effects=True, vmem_limit_bytes=56 << 20
            ),
        )(
            density,
            hamil_dens,
            occupied_p,
            occupied_hp,
            window_sizes,
            row_window_sizes,
            slab_index,
            group_sizes,
        )
        return product, norm.reshape(())

    return jax.shard_map(
        per_device,
        mesh=mesh,
        in_specs=(
            P("blk", None),
            P("blk", None),
            P("blk", "col"),
            P("blk", "col"),
            P(),
            P(),
            P("col"),
            P(),
        ),
        out_specs=(P("blk", "col"), P()),
        check_vma=False,
    )
```

```python
import functools

import jax
import jax.numpy as jnp
from jax import lax
from jax.experimental import pallas as pl
from jax.experimental.pallas import tpu as pltpu
from jax.sharding import PartitionSpec as P

MESH = pl.DeviceIdType.MESH
PAIR = 2
CHUNKS = 4
EXTRA = 1


def kernel(
    length,
    cols,
    density,
    hamil_in,
    occ_p_in,
    occ_hp_in,
    window_in,
    row_window_in,
    slab_in,
    groups_in,
    product_out,
    norm,
    product,
    hamil,
    occ_p,
    occ_hp,
    window,
    row_window,
    slab,
    groups,
    gathered,
    p_in,
    p_high,
    p_low,
    parts,
    col_parts,
    send_sem,
    recv_sem,
    load_sem,
    part_send,
    part_recv,
    col_send,
    col_recv,
):
    count = length * PAIR
    block, width = hamil.shape
    row_blocks = product.shape[0] // block
    panels = width // block
    piece = block // CHUNKS
    me = lax.axis_index("blk")
    my_col = lax.axis_index("col")
    z = me // PAIR
    x = me % PAIR
    partner = me + 1 - 2 * x
    has_up = z < length - 1
    has_down = z > 0

    loads = [
        pltpu.make_async_copy(source, target, load_sem.at[at])
        for at, (source, target) in enumerate(
            (
                (hamil_in, hamil),
                (occ_hp_in, occ_hp),
                (window_in, window),
                (slab_in, slab),
                (groups_in, groups),
                (row_window_in, row_window),
                (occ_p_in, occ_p),
                (density, p_in),
            )
        )
    ]
    barrier = pltpu.get_barrier_semaphore()

    @pl.loop(1, count)
    def greet_blk(step):
        pl.semaphore_signal(
            barrier, inc=1, device_id={"blk": (me + step) % count}, device_id_type=MESH
        )

    @pl.loop(1, cols)
    def greet_col(step):
        pl.semaphore_signal(
            barrier, inc=1, device_id={"col": (my_col + step) % cols}, device_id_type=MESH
        )

    for load in loads:
        load.start()

    for load in loads[:5]:
        load.wait()

    row_at = lax.broadcasted_iota(jnp.int32, (block, block), 0)
    col_at = lax.broadcasted_iota(jnp.int32, (block, block), 1)
    rows_live = row_at < window[me]
    for panel in range(panels):
        size = groups[slab[panel]]
        occupied = occ_hp[0, panel].astype(jnp.float32)
        mask = jnp.where(rows_live & (col_at < size), occupied, 0.0)
        here = pl.ds(panel * block, block)
        gathered[me, :, here] = hamil[:, here] * mask

    pl.semaphore_wait(barrier, count - 1 + cols - 1)

    def move(where, k, chunk, device):
        rows = gathered.at[k, pl.ds(chunk * piece, piece), :]
        return pltpu.make_async_remote_copy(
            src_ref=rows,
            dst_ref=rows,
            send_sem=send_sem.at[where, k, chunk],
            recv_sem=recv_sem.at[k, chunk],
            device_id={"blk": device},
            device_id_type=MESH,
        )

    def up(k, chunk):
        return move(0, k, chunk, me + PAIR)

    def down(k, chunk):
        return move(1, k, chunk, me - PAIR)

    def across(k, chunk):
        return move(2, k, chunk, partner)

    for chunk in range(CHUNKS):
        across(me, chunk).start()

        @pl.when(has_up)
        def _():
            up(me, chunk).start()

        @pl.when(has_down)
        def _():
            down(me, chunk).start()

    for load in loads[5:]:
        load.wait()

    @pl.loop(0, length)
    def split(at):
        for b in range(row_blocks):
            live = row_at < row_window[me * row_blocks + b]
            here = pl.ds(b * block, block)
            for other in range(PAIR):
                k = at * PAIR + other
                mask = jnp.where(
                    live & (col_at < window[k]), occ_p[b, k].astype(jnp.float32), 0.0
                )
                value = p_in[here, pl.ds(pl.multiple_of(k * block, block), block)] * mask
                high = value.astype(jnp.bfloat16)
                there = pl.ds(other * block, block)
                p_high[at, here, there] = high
                p_low[at, here, there] = (value - high.astype(jnp.float32)).astype(jnp.bfloat16)

    def term(at, first):
        right = gathered[pl.ds(at * PAIR, PAIR)].reshape(PAIR * block, width)
        high = right.astype(jnp.bfloat16)
        low = (right - high.astype(jnp.float32)).astype(jnp.bfloat16)

        def times(a, b):
            return jnp.dot(a, b, preferred_element_type=jnp.float32)

        left = p_high[at]
        value = times(left, low) + times(p_low[at], high) + times(left, high)
        product[...] = value if first else product[...] + value

    for chunk in range(EXTRA):
        across(partner, chunk).wait_recv()

        @pl.when(has_up)
        def _():
            up(partner, chunk).start()

        @pl.when(has_down)
        def _():
            down(partner, chunk).start()

    def pass_on(distance):
        for chunk in range(CHUNKS):

            @pl.when(z - distance >= 0)
            def _():
                k = me - distance * PAIR
                across(k, chunk).wait_recv()

                @pl.when(has_up)
                def _():
                    up(k, chunk).start()

                if chunk < EXTRA:

                    @pl.when(distance > 1)
                    def _():
                        across(k, chunk).start()

                else:
                    across(k, chunk).start()

            @pl.when(z + distance < length)
            def _():
                k = me + distance * PAIR
                across(k, chunk).wait_recv()

                @pl.when(has_down)
                def _():
                    down(k, chunk).start()

                if chunk < EXTRA:

                    @pl.when(distance > 1)
                    def _():
                        across(k, chunk).start()

                else:
                    across(k, chunk).start()

    def add_terms(distance):
        for sign in (-1, 1):
            at = z + sign * distance

            @pl.when((at >= 0) & (at < length))
            def _():
                for chunk in range(CHUNKS):
                    across(partner + sign * distance * PAIR, chunk).wait_recv()
                term(at, False)

    if length > 1:
        pass_on(1)

    for chunk in range(EXTRA, CHUNKS):
        across(partner, chunk).wait_recv()
    term(z, True)

    @pl.loop(2, length)
    def steps(distance):
        pass_on(distance)

    @pl.loop(1, length)
    def products(distance):
        add_terms(distance)

    store = pltpu.make_async_copy(product, product_out, load_sem.at[0])
    store.start()

    squares = product[...] * product[...]
    squares = jnp.sum(squares.reshape(squares.shape[0] // 8, 8, width), axis=0)
    total = squares[:, :128]
    for panel in range(1, width // 128):
        total = total + squares[:, panel * 128 : (panel + 1) * 128]
    parts[me] = total

    def part_to(device):
        return pltpu.make_async_remote_copy(
            src_ref=parts.at[me],
            dst_ref=parts.at[me],
            send_sem=part_send.at[device],
            recv_sem=part_recv.at[me],
            device_id={"blk": device},
            device_id_type=MESH,
        )

    def part_from(device):
        return pltpu.make_async_remote_copy(
            src_ref=parts.at[device],
            dst_ref=parts.at[device],
            send_sem=part_send.at[device],
            recv_sem=part_recv.at[device],
            device_id={"blk": device},
            device_id_type=MESH,
        )

    @pl.loop(1, count)
    def send_parts(step):
        part_to((me + step) % count).start()

    @pl.loop(0, length)
    def sent(at):
        k = at * PAIR + x
        far = (at - z > 1) | (z - at > 1) | (at == z)
        for chunk in range(CHUNKS):

            @pl.when(has_up & (at <= z))
            def _():
                up(k, chunk).wait_send()

            @pl.when(has_down & (at >= z))
            def _():
                down(k, chunk).wait_send()

            if chunk < EXTRA:

                @pl.when(far)
                def _():
                    across(k, chunk).wait_send()

            else:
                across(k, chunk).wait_send()

    for chunk in range(EXTRA):

        @pl.when(has_up)
        def _():
            up(partner, chunk).wait_send()

        @pl.when(has_down)
        def _():
            down(partner, chunk).wait_send()

    @pl.loop(1, count)
    def get_parts(step):
        part_from((me + step) % count).wait_recv()

    col_parts[my_col] = jnp.sum(parts[...], axis=0)

    def col_to(device):
        return pltpu.make_async_remote_copy(
            src_ref=col_parts.at[my_col],
            dst_ref=col_parts.at[my_col],
            send_sem=col_send.at[device],
            recv_sem=col_recv.at[my_col],
            device_id={"col": device},
            device_id_type=MESH,
        )

    def col_from(device):
        return pltpu.make_async_remote_copy(
            src_ref=col_parts.at[device],
            dst_ref=col_parts.at[device],
            send_sem=col_send.at[device],
            recv_sem=col_recv.at[device],
            device_id={"col": device},
            device_id_type=MESH,
        )

    @pl.loop(1, cols)
    def send_cols(step):
        col_to((my_col + step) % cols).start()

    @pl.loop(1, count)
    def sent_parts(step):
        part_to((me + step) % count).wait_send()

    @pl.loop(1, cols)
    def get_cols(step):
        col_from((my_col + step) % cols).wait_recv()

    store.wait()
    norm[0] = jnp.sum(jnp.sum(col_parts[...], axis=0))

    @pl.loop(1, cols)
    def sent_cols(step):
        col_to((my_col + step) % cols).wait_send()


def solution(mesh):
    count = mesh.shape["blk"]
    cols = mesh.shape["col"]
    length = count // PAIR

    def per_device(
        density,
        occupied_p,
        hamil_dens,
        occupied_hp,
        window_sizes,
        row_window_sizes,
        slab_index,
        group_sizes,
    ):
        rows, inner = density.shape
        block, width = hamil_dens.shape
        hbm = pl.BlockSpec(memory_space=pltpu.HBM)
        smem = pl.BlockSpec(memory_space=pltpu.SMEM)
        product, norm = pl.pallas_call(
            functools.partial(kernel, length, cols),
            out_shape=(
                jax.ShapeDtypeStruct((rows, width), jnp.float32),
                jax.ShapeDtypeStruct((1,), jnp.float32),
            ),
            in_specs=[hbm] * 8,
            out_specs=(hbm, smem),
            scratch_shapes=[
                pltpu.VMEM((rows, width), jnp.float32),
                pltpu.VMEM((block, width), jnp.float32),
                pltpu.SMEM(occupied_p.shape, jnp.int32),
                pltpu.SMEM(occupied_hp.shape, jnp.int32),
                pltpu.SMEM(window_sizes.shape, jnp.int32),
                pltpu.SMEM(row_window_sizes.shape, jnp.int32),
                pltpu.SMEM(slab_index.shape, jnp.int32),
                pltpu.SMEM(group_sizes.shape, jnp.int32),
                pltpu.VMEM((count, block, width), jnp.float32),
                pltpu.VMEM((rows, inner), jnp.float32),
                pltpu.VMEM((length, rows, PAIR * block), jnp.bfloat16),
                pltpu.VMEM((length, rows, PAIR * block), jnp.bfloat16),
                pltpu.VMEM((count, 8, 128), jnp.float32),
                pltpu.VMEM((cols, 8, 128), jnp.float32),
                pltpu.SemaphoreType.DMA((3, count, CHUNKS)),
                pltpu.SemaphoreType.DMA((count, CHUNKS)),
                pltpu.SemaphoreType.DMA((8,)),
                pltpu.SemaphoreType.DMA((count,)),
                pltpu.SemaphoreType.DMA((count,)),
                pltpu.SemaphoreType.DMA((cols,)),
                pltpu.SemaphoreType.DMA((cols,)),
            ],
            compiler_params=pltpu.CompilerParams(
                collective_id=0, has_side_effects=True, vmem_limit_bytes=56 << 20
            ),
        )(
            density,
            hamil_dens,
            occupied_p,
            occupied_hp,
            window_sizes,
            row_window_sizes,
            slab_index,
            group_sizes,
        )
        return product, norm.reshape(())

    return jax.shard_map(
        per_device,
        mesh=mesh,
        in_specs=(
            P("blk", None),
            P("blk", None),
            P("blk", "col"),
            P("blk", "col"),
            P(),
            P(),
            P("col"),
            P(),
        ),
        out_specs=(P("blk", "col"), P()),
        check_vma=False,
    )
```
